32 devices in a mesh: parts: 2 (over y), dp: 4 (over z), tensor: 2 (over x), seq: 2 (over core).
Axes of the slice: x: 2, y: 2, z: 4, core: 2. Of those that a mesh axis runs over, the one named last changes fastest.
Arguments:
- acts: bfloat16 [8192, 8192], P(('parts', 'dp', 'seq'), 'tensor'), parts along dimension 0, may hold values from -6 to 6
- grads: bfloat16 [8192, 32768], P(('parts', 'dp', 'seq'), 'tensor'), parts along dimension 0, may hold values from -0.029907227 to 0.029907227
- eig_in: bfloat16 [8192, 512], P('tensor'), may hold values from -0.0625 to 0.0625
- eig_out: bfloat16 [32768, 256], P('tensor'), may hold values from -0.03125 to 0.03125
- query_acts: bfloat16 [4096, 8192], P(('parts', 'dp', 'seq'), 'tensor'), parts along dimension 0, may hold values from -6 to 6
- query_grads: bfloat16 [4096, 32768], P(('parts', 'dp', 'seq'), 'tensor'), parts along dimension 0, may hold values from -0.029907227 to 0.029907227
- eigenvalues: float32 [256, 512], P('tensor'), may hold values from 0.05 to 5
- lengths: int32 [8, 16], P(('parts', 'dp')), parts along dimension 0, may hold values from 1 to 256, 1024 in all within a row
- owner: int32 [8, 16, 1], P(('parts', 'dp')), parts along dimension 0, may hold values from 0 to 3; in each aligned block of 16 rows (0 to 15, 16 to 31, ..., all dimensions but the last counted through in order) at most 4 rows name the same one
Outputs:
- doc_scores: float32 [128, 64], P(('parts', 'dp'), ('tensor', 'seq')), parts along dimension 0
The draws below stay inside these ranges and needn't reach their ends.
There are 2 independent parts, one for each index of `parts`. The reference program is written for one: setup_inputs(seed, part) draws one part's arguments, and reference() takes and returns one part's arrays. A program takes and returns all parts, laid end to end along the dimension named above; an argument that names none is the same for every part. Nothing has to cross between parts.
Inputs may be any that keep to these rules, and one draw needn't show every extreme that they name: `lengths`: each row gives, in order, the token counts of the 16 documents of one packed sequence; a row sums to 1024. The documents of one sequence name any one owner at most 4 times; in some sequences an owner is named exactly 4 times.
All inputs are finite; a program needn't handle non-finite values.
Results may differ from the reference program's by a relative error of at most 0.0065.
Values may be sent and summed in bfloat16 or wider, within the bound.
A program may use at most 128 MiB of HBM per device.

```python
import math
import jax
import jax.numpy as jnp
import numpy as np
from jax import lax

DIN = 8192
DOUT = 32768
KA = 512
KS = 256
QUERIES = 64
QTOK = 32
DOC_SEQ = 16
SEQ_LEN = 1024
MOST_LEN = 256
TOKENS = 4096
QROWS = 2048
CAP = 4
N_DP = 4


def block_levels(own_key, extent, shards, smallest, top_value):
    def one(axis_at, parts):
        heights = jax.random.uniform(jax.random.fold_in(jax.random.fold_in(own_key, 6), axis_at), (parts,), jnp.float32, smallest / len(shards), top_value / len(shards))
        return jnp.repeat(jnp.exp(heights), extent[axis_at] // parts).reshape((-1,) + (1,) * (len(extent) - axis_at - 1))

    gain = one(*shards[0])
    for cut in shards[1:]:
        gain = gain * one(*cut)
    return gain


def profile(amount, total, limit, lean):
    weights = [(1 << 20) // math.isqrt(grade ** lean) + 1 for grade in range(2, amount + 1)]
    spare, counts = total - limit - (amount - 1), [1] * (amount - 1)
    while spare > 0:
        free = [i for i in range(amount - 1) if counts[i] < limit]
        mass, remaining = sum([weights[i] for i in free]), spare
        for i in free:
            more = min(limit - counts[i], max(1, remaining * weights[i] // mass), spare)
            counts[i] = counts[i] + more
            spare = spare - more
    return np.array([limit] + counts)


def uneven_parts(rng, number_of, total, reach, slope):
    if number_of == 2:
        one = jax.random.randint(rng, (), max(1, total - reach), min(reach, total - 1) + 1)
        return jnp.stack([one, total - one])
    tallies = jnp.asarray(profile(number_of, total, reach, slope), jnp.int32)
    pairs = (number_of - 1) // 2
    giver, sink = tallies[1:1 + 2 * pairs:2], tallies[2:2 + 2 * pairs:2]
    room = jnp.minimum(giver - 1, reach - sink)
    shifted = jax.random.randint(jax.random.fold_in(rng, 1), (pairs,), 0, 1 << 20) % (room + 1)
    tallies = tallies.at[1:1 + 2 * pairs:2].set(giver - shifted).at[2:2 + 2 * pairs:2].set(sink + shifted)
    return tallies[jax.random.permutation(jax.random.fold_in(rng, 2), number_of)]


def routed_block(key, own, number, rows, amount, top, reach, lean):
    sequence = jax.random.permutation(key, amount)
    packed, usual = portions_of(amount, rows * top, reach, lean, True), portions_of(amount, rows * top, reach, lean, False)
    places = jnp.arange(amount)

    def named(tallies, offset_by):
        used = int((tallies > 0).sum())
        fixed = max(1, used // 4)
        shifted = fixed + (places - fixed + offset_by * (used - fixed)) % max(1, amount - fixed)
        return jnp.zeros((amount,), jnp.int32).at[sequence[jnp.where(places < fixed, places, shifted)]].set(jnp.asarray(tallies, jnp.int32))

    tallies = jnp.where(number % 4 == 0, named(packed, number // 4), named(usual, number - number // 4 - 1))
    mixed = jax.random.permutation(jax.random.fold_in(own, 3), amount)
    donor, taker = mixed[0:amount // 2 * 2:2], mixed[1:amount // 2 * 2:2]
    room = jnp.minimum(tallies[donor] - 1, reach - tallies[taker]) // 2
    room = jnp.where((donor == sequence[0]) | (taker == sequence[0]) | (tallies[taker] == 0), 0, jnp.maximum(room, 0))
    shifted = jax.random.randint(jax.random.fold_in(own, 4), (amount // 2,), 0, 1 << 20) % (room + 1)
    tallies = tallies.at[donor].add(-shifted).at[taker].add(shifted)
    items = jnp.searchsorted(jnp.cumsum(tallies), jnp.arange(rows * top), side="right").astype(jnp.int32)
    table = items.reshape(top, rows).T
    table = table[jax.random.permutation(jax.random.fold_in(own, 1), rows)]
    offset_by = jax.random.randint(jax.random.fold_in(own, 2), (rows, 1), 0, top)
    return jnp.take_along_axis(table, (jnp.arange(top)[None, :] + offset_by) % top, axis=1)


def portions_of(number_of, total, bound, slope, full):
    weights = [(1 << 20) // math.isqrt(standing ** slope) + 1 for standing in range(1, number_of + 1)]
    largest = bound if full else min(bound, max(-(-total // number_of), total * weights[0] // sum(weights)))
    least = 1 if total - largest >= number_of - 1 else 0
    counts, rest = [largest] + [least] * (number_of - 1), total - largest - least * (number_of - 1)
    while rest > 0:
        candidates = [i for i in range(1, number_of) if counts[i] < largest] or [i for i in range(1, number_of) if counts[i] < bound]
        mass, remaining = sum([weights[i] for i in candidates]), rest
        for i in candidates:
            more = min(bound - counts[i], max(1, remaining * weights[i] // mass), rest)
            counts[i] = counts[i] + more
            rest = rest - more
    return np.array(counts)


def noise(own_key, shape, scale, limit, shards=(), held_as=jnp.bfloat16):
    result = scale * jax.random.normal(own_key, shape, jnp.float32)
    if shards:
        result = result * block_levels(own_key, shape, shards, -0.22, 0.18)
    return jnp.clip(result, -limit, limit).astype(held_as)


def setup_inputs(seed: int = 0, part: int = 0) -> dict:
    keys = jax.random.split(jax.random.key(seed), 10)
    part_splits = jax.random.split(jax.random.fold_in(keys[9], part), 10)
    acts = noise(part_splits[0], (TOKENS, DIN), 1.0, 6.0, ((0, 8), (1, 2)))
    grads = noise(part_splits[1], (TOKENS, DOUT), 0.005, 0.029907227, ((0, 8), (1, 2)))
    eig_in = noise(keys[2], (DIN, KA), DIN ** -0.5, 0.0625, ((0, 2),))
    eig_out = noise(keys[3], (DOUT, KS), DOUT ** -0.5, 0.03125, ((0, 2),))
    query_acts = noise(part_splits[4], (QROWS, DIN), 1.0, 6.0, ((0, 8), (1, 2)))
    query_grads = noise(part_splits[5], (QROWS, DOUT), 0.005, 0.029907227, ((0, 8), (1, 2)))
    eigenvalues = jnp.clip(jnp.exp(math.log(5.0) - 4.6051702 * jax.random.uniform(keys[6], (KS, KA), jnp.float32) ** block_levels(keys[6], (KS, KA), ((0, 2),), -0.2, 0.2)), 0.05, 5.0)
    lengths = jax.vmap(lambda own: uneven_parts(own, DOC_SEQ, SEQ_LEN, MOST_LEN, 2))(jax.random.split(part_splits[7], N_DP)).reshape((N_DP, DOC_SEQ)).astype(jnp.int32)
    owner_keys = jax.random.split(jax.random.fold_in(part_splits[8], 1), N_DP * DOC_SEQ // DOC_SEQ)
    owner_turns = jax.random.permutation(jax.random.fold_in(part_splits[8], 3), N_DP * DOC_SEQ // DOC_SEQ)
    owner = jax.vmap(lambda own, number: routed_block(jax.random.fold_in(part_splits[8], 2), own, number, DOC_SEQ, N_DP, 1, CAP, 2))(owner_keys, owner_turns).reshape((N_DP, DOC_SEQ, 1))
    return {"acts": acts, "grads": grads, "eig_in": eig_in, "eig_out": eig_out, "query_acts": query_acts, "query_grads": query_grads, "eigenvalues": eigenvalues, "lengths": lengths, "owner": owner}


damping = 0.01


def reference(acts, grads, eig_in, eig_out, query_acts, query_grads, eigenvalues, lengths, owner):
    highest = lax.Precision.HIGHEST
    in_rot = jnp.dot(acts, eig_in, preferred_element_type=jnp.float32).astype(jnp.bfloat16)
    out_rot = jnp.dot(grads, eig_out, preferred_element_type=jnp.float32).astype(jnp.bfloat16)
    query_in = jnp.dot(query_acts, eig_in, preferred_element_type=jnp.float32).astype(jnp.bfloat16)
    query_out = jnp.dot(query_grads, eig_out, preferred_element_type=jnp.float32).astype(jnp.bfloat16)
    left_side = query_out.astype(jnp.float32).reshape(QUERIES, QTOK, KS)
    right_side = query_in.astype(jnp.float32).reshape(QUERIES, QTOK, KA)
    outer_sum = jnp.einsum("qui,quj->qij", left_side, right_side, precision=highest)
    damped = (outer_sum / (eigenvalues + damping)).astype(jnp.bfloat16)
    damped_flat = damped.astype(jnp.float32).reshape(QUERIES * KS, KA)

    def one_sequence(items):
        seq_in, seq_out, doc_lengths = items
        spread = lax.dot_general(seq_in.astype(jnp.float32), damped_flat, (((1,), (1,)), ((), ())), precision=highest)
        scores = jnp.sum(spread.reshape(SEQ_LEN, QUERIES, KS) * seq_out.astype(jnp.float32)[:, None, :], axis=2)
        doc_ends = jnp.cumsum(doc_lengths)
        doc_begins = doc_ends - doc_lengths
        positions = jnp.arange(SEQ_LEN, dtype=jnp.int32)
        member = ((positions[:, None] >= doc_begins[None, :]) & (positions[:, None] < doc_ends[None, :])).astype(jnp.float32)
        return lax.dot_general(member, scores, (((0,), (0,)), ((), ())), precision=highest)

    local_scores = lax.map(one_sequence, (in_rot.reshape(N_DP, SEQ_LEN, KA), out_rot.reshape(N_DP, SEQ_LEN, KS), lengths))
    doc_order = jnp.arange(DOC_SEQ, dtype=jnp.int32)
    doc_owner = owner[:, :, 0].astype(jnp.int32)
    earlier = (doc_owner[:, None, :] == doc_owner[:, :, None]) & (doc_order[None, None, :] < doc_order[None, :, None])
    doc_slot = jnp.sum(earlier.astype(jnp.int32), axis=2).astype(jnp.int32)
    sources = jnp.arange(N_DP, dtype=jnp.int32)[:, None]
    target = ((doc_owner * N_DP + sources) * CAP + doc_slot).astype(jnp.int32)
    owned_table = jnp.zeros((N_DP * N_DP * CAP, QUERIES), jnp.float32)
    return owned_table.at[target.reshape(-1)].set(local_scores.reshape(N_DP * DOC_SEQ, QUERIES))
```

```python
import functools

import jax
import jax.numpy as jnp
from jax import lax
from jax.experimental import pallas as pl
from jax.experimental.pallas import tpu as pltpu
from jax.sharding import PartitionSpec as P

QTOK = 32
PAD = 8
LANES = 128
GROUP = 16


damping = 0.01
MESH = pl.DeviceIdType.MESH
f32, bf16 = jnp.float32, jnp.bfloat16


def dot(a, b, dims=((1,), (0,)), precision=None):
    return lax.dot_general(a, b, (dims, ((), ())), precision=precision, preferred_element_type=f32)


def kernel(
    sizes, len_ref, own_ref, acts, grads, eig_in, eig_out, query_acts, query_grads, eigenvalues, out_ref,
    v_a, v_g, v_ei, v_eo, v_qa, v_qg,
    acc_ti, acc_to, acc_qi, acc_qo,
    send_ti, send_to, send_qi, send_qo,
    got_ti, got_to, got_qi, got_qo,
    tok_in, tok_out, que_in, que_out,
    levels, doc_grad, que_grad, pair, placed, table,
    load_sem, x_send, x_recv, core_send, core_recv, z_send, z_recv, last_send, last_recv,
):
    nz, nx, n_in, n_out, in_step, out_step, doc_count, capacity = sizes
    part, z, x, s = (lax.axis_index(name) for name in ("parts", "dp", "tensor", "seq"))
    n_all = nz * nx * 2
    me = (z * nx + x) * 2 + s
    rows, wide = acc_ti.shape[1:]
    ks = acc_to.shape[1]
    q_rows = acc_qo.shape[0]
    q_each = q_rows // QTOK
    q_all = nz * q_each

    def place(index):
        return lax.div(index, 2 * nx), lax.rem(lax.div(index, 2), nx), lax.rem(index, 2)

    def load(kind, c):
        src, dst = {
            "eo": lambda: (eig_out.at[pl.ds(c * out_step, out_step), :], v_eo.at[c]),
            "qg": lambda: (query_grads.at[:, pl.ds(c * out_step, out_step)], v_qg.at[c]),
            "g": lambda: (grads.at[:, pl.ds(c * out_step, out_step)], v_g.at[c]),
            "ei": lambda: (eig_in.at[pl.ds(c * in_step, in_step), :], v_ei.at[c]),
            "qa": lambda: (query_acts.at[:, pl.ds(c * in_step, in_step)], v_qa.at[c]),
            "a": lambda: (acts.at[:, pl.ds(c * in_step, in_step)], v_a.at[c]),
        }[kind]()
        row = ("eo", "qg", "g", "ei", "qa", "a").index(kind)
        return pltpu.make_async_copy(src, dst, load_sem.at[row, c])

    for c in range(n_out):
        load("eo", c).start()
        load("qg", c).start()
    for c in range(n_in):
        load("ei", c).start()
        load("qa", c).start()
    for c in range(n_out):
        load("g", c).start()
    for c in range(n_in):
        load("a", c).start()
    own_level = pltpu.make_async_copy(
        eigenvalues.at[:, pl.ds(pl.multiple_of(x * wide, LANES), wide)], levels.at[x], load_sem.at[6, 0]
    )
    own_level.start()

    barrier = pltpu.get_barrier_semaphore()

    def greet(r, carry):
        oz, ox, os = place(lax.rem(me + r, n_all))
        pl.semaphore_signal(barrier, inc=1, device_id=(part, oz, ox, os), device_id_type=MESH)
        return carry

    lax.fori_loop(1, n_all, greet, 0)

    def along_x(kind, r, arriving=False):
        other = lax.rem(x + r, nx)
        back = lax.rem(x + nx - r, nx)
        src, dst = {
            "ev": lambda: (eigenvalues.at[:, pl.ds(pl.multiple_of(other * wide, LANES), wide)], levels),
            "qi": lambda: (send_qi.at[other], got_qi),
            "qo": lambda: (send_qo, got_qo),
            "ti": lambda: (send_ti.at[other], got_ti),
            "to": lambda: (send_to, got_to),
        }[kind]()
        row = ("ev", "qi", "qo", "ti", "to").index(kind)

        def copy(slot):
            return pltpu.make_async_remote_copy(
                src_ref=src, dst_ref=dst.at[slot], send_sem=x_send.at[row, r], recv_sem=x_recv.at[row, r],
                device_id=(part, z, other, s), device_id_type=MESH,
            )

        return copy(back if arriving else x)

    def start_x(kind):
        for r in range(1, nx):
            along_x(kind, r).start()

    def wait_x(kind):
        for r in range(1, nx):
            along_x(kind, r, True).wait_recv()

    def summed(own, got):
        total = own
        for r in range(1, nx):
            total = total + got[lax.rem(x + nx - r, nx)].astype(f32)
        return total

    def rotate_out(kind, held, acc):
        acc[...] = jnp.zeros_like(acc)

        def step(c, carry):
            if kind == "qg":
                load("eo", c).wait()
            load(kind, c).wait()
            acc[...] += dot(held[c], v_eo[c])
            return carry

        lax.fori_loop(0, n_out, step, 0)

    def rotate_in(kind, held, acc):
        acc[...] = jnp.zeros_like(acc)

        def step(c, carry):
            if kind == "qa":
                load("ei", c).wait()
            load(kind, c).wait()
            for j in range(nx):
                acc[j] += dot(held[c], v_ei[c, :, j * wide:(j + 1) * wide])
            return carry

        lax.fori_loop(0, n_in, step, 0)

    rotate_out("qg", v_qg, acc_qo)
    send_qo[...] = acc_qo[...].astype(bf16)
    pl.semaphore_wait(barrier, n_all - 1)
    start_x("ev")
    start_x("qo")
    rotate_in("qa", v_qa, acc_qi)
    send_qi[...] = acc_qi[...].astype(bf16)
    start_x("qi")

    rotate_out("g", v_g, acc_to)
    send_to[...] = acc_to[...].astype(bf16)
    start_x("to")

    def along_z(kind, r, arriving=False):
        ref = que_out if kind == 0 else que_in
        other = lax.rem(z + r, nz)
        back = lax.rem(z + nz - r, nz)

        def copy(slot):
            return pltpu.make_async_remote_copy(
                src_ref=ref.at[slot], dst_ref=ref.at[slot], send_sem=z_send.at[kind, r], recv_sem=z_recv.at[kind, r],
                device_id=(part, other, x, s), device_id_type=MESH,
            )

        return copy(back if arriving else z)

    wait_x("qo")
    que_out[z] = summed(acc_qo[...], got_qo).T.astype(bf16)
    wait_x("qi")
    que_in[z] = summed(acc_qi[x], got_qi).astype(bf16)

    def start_z(r, carry):
        along_z(0, r).start()
        along_z(1, r).start()
        return carry

    lax.fori_loop(1, nz, start_z, 0)

    rotate_in("a", v_a, acc_ti)
    send_ti[...] = acc_ti[...].astype(bf16)
    start_x("ti")

    own_level.wait()
    wait_x("ev")
    levels[...] = 1.0 / (levels[...] + damping)

    def damp(zb):
        lane = lax.broadcasted_iota(jnp.int32, (1, q_rows), 1)
        scale = levels[...].reshape(ks, wide)

        def one(k, carry):
            keep = ((lane >= k * QTOK) & (lane < (k + 1) * QTOK)).astype(f32).astype(bf16)
            outer = dot(que_out[zb] * keep, que_in[zb])
            que_grad[:, zb * q_each + k] = (outer * scale).astype(bf16).reshape(ks // GROUP, GROUP, wide)
            return carry

        lax.fori_loop(0, q_each, one, 0)

    damp(z)

    def to_core(kind, slot):
        ref = tok_out if kind == 0 else tok_in
        return pltpu.make_async_remote_copy(
            src_ref=ref.at[slot], dst_ref=ref.at[slot], send_sem=core_send.at[kind], recv_sem=core_recv.at[kind],
            device_id=(part, z, x, 1 - s), device_id_type=MESH,
        )

    wait_x("to")
    tok_out[s] = summed(acc_to[...], got_to).T.astype(bf16)
    to_core(0, s).start()
    wait_x("ti")
    tok_in[s] = summed(acc_ti[x], got_ti).astype(bf16)
    to_core(1, s).start()
    to_core(0, 1 - s).wait_recv()
    to_core(1, 1 - s).wait_recv()

    def document(d, begin):
        end = begin + len_ref[0, d]
        total = None
        for half in range(2):
            at = lax.broadcasted_iota(jnp.int32, (1, rows), 1) + half * rows
            keep = ((at >= begin) & (at < end)).astype(f32).astype(bf16)
            term = dot(tok_out[half] * keep, tok_in[half])
            total = term if total is None else total + term
        doc_grad[:, d] = total.astype(bf16).reshape(ks // GROUP, GROUP, wide)
        return end

    lax.fori_loop(0, doc_count, document, jnp.int32(0))

    def damp_far(r, carry):
        along_z(0, r, True).wait_recv()
        along_z(1, r, True).wait_recv()
        damp(lax.rem(z + nz - r, nz))
        return carry

    lax.fori_loop(1, nz, damp_far, 0)

    pair[...] = jnp.zeros_like(pair)

    def pairs(g, carry):
        left = doc_grad[g].reshape(doc_count * GROUP, wide)
        right = que_grad[g].reshape(q_all * GROUP, wide)
        pair[...] += dot(left, right, ((1,), (1,)))
        return carry

    lax.fori_loop(0, ks // GROUP, pairs, 0)
    row = lax.broadcasted_iota(jnp.int32, pair.shape, 0)
    col = lax.broadcasted_iota(jnp.int32, pair.shape, 1)
    same = jnp.where(lax.rem(row, GROUP) == lax.rem(col, GROUP), pair[...], 0.0)
    by_doc = jnp.sum(same.reshape(doc_count, GROUP, q_all * GROUP), axis=1)
    fold_row = lax.broadcasted_iota(jnp.int32, (q_all * GROUP, LANES), 0)
    fold_col = lax.broadcasted_iota(jnp.int32, (q_all * GROUP, LANES), 1)
    fold = (lax.div(fold_row, GROUP) == fold_col).astype(f32)
    highest = lax.Precision.HIGHEST
    scores = dot(by_doc, fold, precision=highest)

    slot_row = lax.broadcasted_iota(jnp.int32, (nz * PAD, doc_count), 0)
    slot_col = lax.broadcasted_iota(jnp.int32, (nz * PAD, doc_count), 1)
    placing = jnp.zeros((nz * PAD, doc_count), f32)
    for d in range(doc_count):
        owner = own_ref[0, d]
        slot = jnp.int32(0)
        for e in range(d):
            slot = slot + jnp.where(own_ref[0, e] == owner, 1, 0)
        placing = jnp.where((slot_row == owner * PAD + slot) & (slot_col == d), 1.0, placing)
    placed[...] = dot(placing, scores, precision=highest).reshape(nz, PAD, LANES)

    def to_owner(r):
        oz, ox, os = place(lax.rem(me + r, n_all))
        return pltpu.make_async_remote_copy(
            src_ref=placed.at[oz], dst_ref=table.at[x * 2 + s, z], send_sem=last_send.at[r], recv_sem=last_recv.at[r],
            device_id=(part, oz, ox, os), device_id_type=MESH,
        )

    def from_source(r):
        oz, ox, os = place(lax.rem(me + n_all - r, n_all))
        return pltpu.make_async_remote_copy(
            src_ref=placed.at[0], dst_ref=table.at[ox * 2 + os, oz], send_sem=last_send.at[r], recv_sem=last_recv.at[r],
            device_id=(part, oz, ox, os), device_id_type=MESH,
        )

    def start_last(r, carry):
        to_owner(r).start()
        return carry

    lax.fori_loop(1, n_all, start_last, 0)
    table[x * 2 + s, z] = placed[z]

    for kind in ("ev", "qi", "qo", "ti", "to"):
        for r in range(1, nx):
            along_x(kind, r).wait_send()
    to_core(0, s).wait_send()
    to_core(1, s).wait_send()

    def sent_z(r, carry):
        along_z(0, r).wait_send()
        along_z(1, r).wait_send()
        return carry

    lax.fori_loop(1, nz, sent_z, 0)

    def finish_last(r, carry):
        from_source(r).wait_recv()
        to_owner(r).wait_send()
        return carry

    lax.fori_loop(1, n_all, finish_last, 0)

    width = out_ref.shape[1]
    block = x * 2 + s
    result = jnp.zeros((nz * PAD, width), f32)
    pick_row = lax.broadcasted_iota(jnp.int32, (LANES, width), 0)
    pick_col = lax.broadcasted_iota(jnp.int32, (LANES, width), 1)
    for side in range(2):
        total = table[side].reshape(nz * PAD, LANES)
        for ox in range(1, nx):
            total = total + table[ox * 2 + side].reshape(nz * PAD, LANES)
        query = lax.div(pick_row, q_each) * (2 * q_each) + side * q_each + lax.rem(pick_row, q_each)
        pick = ((query == block * width + pick_col) & (pick_row < q_all)).astype(f32)
        result = result + dot(total, pick, precision=highest)
    for zz in range(nz):
        out_ref[zz * capacity:(zz + 1) * capacity, :] = result[zz * PAD:zz * PAD + capacity, :]


def chunk(extent, most):
    return min(extent, most)


def per_device(acts, grads, eig_in, eig_out, query_acts, query_grads, eigenvalues, lengths, owner):
    nz, nx = lax.axis_size("dp"), lax.axis_size("tensor")
    rows, q_rows = acts.shape[0], query_acts.shape[0]
    ka, ks = eig_in.shape[1], eig_out.shape[1]
    wide = ka // nx
    in_step, out_step = chunk(acts.shape[1], 2048), chunk(grads.shape[1], 2048)
    n_in, n_out = acts.shape[1] // in_step, grads.shape[1] // out_step
    doc_count = lengths.shape[1]
    capacity = max(3, (doc_count + nz - 1) // nz)
    q_each = q_rows // QTOK
    q_all = nz * q_each
    n_all = nz * nx * 2
    width = q_all * 2 // (nx * 2)
    sizes = (nz, nx, n_in, n_out, in_step, out_step, doc_count, capacity)
    any_spec = pl.BlockSpec(memory_space=pl.ANY)
    smem = pl.BlockSpec(memory_space=pltpu.SMEM)
    dma = pltpu.SemaphoreType.DMA
    return pl.pallas_call(
        functools.partial(kernel, sizes),
        out_shape=jax.ShapeDtypeStruct((nz * capacity, width), f32),
        in_specs=[smem, smem] + [any_spec] * 7,
        out_specs=pl.BlockSpec(memory_space=pltpu.VMEM),
        scratch_shapes=[
            pltpu.VMEM((n_in, rows, in_step), bf16),
            pltpu.VMEM((n_out, rows, out_step), bf16),
            pltpu.VMEM((n_in, in_step, ka), bf16),
            pltpu.VMEM((n_out, out_step, ks), bf16),
            pltpu.VMEM((n_in, q_rows, in_step), bf16),
            pltpu.VMEM((n_out, q_rows, out_step), bf16),
            pltpu.VMEM((nx, rows, wide), f32),
            pltpu.VMEM((rows, ks), f32),
            pltpu.VMEM((nx, q_rows, wide), f32),
            pltpu.VMEM((q_rows, ks), f32),
            pltpu.VMEM((nx, rows, wide), bf16),
            pltpu.VMEM((rows, ks), bf16),
            pltpu.VMEM((nx, q_rows, wide), bf16),
            pltpu.VMEM((q_rows, ks), bf16),
            pltpu.VMEM((nx, rows, wide), bf16),
            pltpu.VMEM((nx, rows, ks), bf16),
            pltpu.VMEM((nx, q_rows, wide), bf16),
            pltpu.VMEM((nx, q_rows, ks), bf16),
            pltpu.VMEM((2, rows, wide), bf16),
            pltpu.VMEM((2, ks, rows), bf16),
            pltpu.VMEM((nz, q_rows, wide), bf16),
            pltpu.VMEM((nz, ks, q_rows), bf16),
            pltpu.VMEM((nx, ks // nx, wide), f32),
            pltpu.VMEM((ks // GROUP, doc_count, GROUP, wide), bf16),
            pltpu.VMEM((ks // GROUP, q_all, GROUP, wide), bf16),
            pltpu.VMEM((doc_count * GROUP, q_all * GROUP), f32),
            pltpu.VMEM((nz, PAD, LANES), f32),
            pltpu.VMEM((nx * 2, nz, PAD, LANES), f32),
            dma((7, max(n_in, n_out))),
            dma((5, nx)),
            dma((5, nx)),
            dma((2,)),
            dma((2,)),
            dma((2, nz)),
            dma((2, nz)),
            dma((n_all,)),
            dma((n_all,)),
        ],
        compiler_params=pltpu.CompilerParams(
            collective_id=0, has_side_effects=True, vmem_limit_bytes=63 * 1024 * 1024
        ),
        cost_estimate=pl.CostEstimate(
            flops=2 * (rows + q_rows) * (acts.shape[1] * ka + grads.shape[1] * ks),
            bytes_accessed=2 * (rows + q_rows) * (acts.shape[1] + grads.shape[1]),
            transcendentals=0,
        ),
    )(
        lengths, owner.reshape(1, doc_count), acts, grads, eig_in, eig_out, query_acts, query_grads, eigenvalues
    )


def solution(mesh):
    return jax.shard_map(
        per_device,
        mesh=mesh,
        in_specs=(
            P(("parts", "dp", "seq"), "tensor"),
            P(("parts", "dp", "seq"), "tensor"),
            P("tensor", None),
            P("tensor", None),
            P(("parts", "dp", "seq"), "tensor"),
            P(("parts", "dp", "seq"), "tensor"),
            P("tensor", None),
            P(("parts", "dp"), None),
            P(("parts", "dp"), None, None),
        ),
        out_specs=P(("parts", "dp"), ("tensor", "seq")),
        check_vma=False,
    )
```

```python
import functools

import jax
import jax.numpy as jnp
from jax import lax
from jax.experimental import pallas as pl
from jax.experimental.pallas import tpu as pltpu
from jax.sharding import PartitionSpec as P

QTOK = 32
PAD = 8
LANES = 128
GROUP = 16


damping = 0.01
MESH = pl.DeviceIdType.MESH
f32, bf16 = jnp.float32, jnp.bfloat16


def dot(a, b, dims=((1,), (0,)), precision=None):
    return lax.dot_general(a, b, (dims, ((), ())), precision=precision, preferred_element_type=f32)


def kernel(
    sizes, len_ref, own_ref, acts, grads, eig_in, eig_out, query_acts, query_grads, eigenvalues, out_ref,
    v_a, v_g0, v_g1, v_ei, v_eo, v_qa, v_qg,
    acc_ti, acc_to0, acc_to1, acc_qi, acc_qo,
    send_ti, send_to0, send_to1, send_qi, send_qo,
    got_ti, got_to0, got_to1, got_qi, got_qo,
    tok_in, tok_out0, tok_out1, que_in, que_out,
    levels, doc_grad, que_grad, pair, fold, placed, table,
    load_sem, x_send, x_recv, core_send, core_recv, z_send, z_recv, last_send, last_recv,
):
    tok_out = (tok_out0, tok_out1)
    nz, nx, n_in, n_out, in_step, out_step, doc_count, capacity = sizes
    part, z, x, s = (lax.axis_index(name) for name in ("parts", "dp", "tensor", "seq"))
    n_all = nz * nx * 2
    me = (z * nx + x) * 2 + s
    rows, wide = acc_ti.shape[1:]
    ks = acc_to0.shape[1]
    half = rows // 2
    q_rows = acc_qo.shape[0]
    q_each = q_rows // QTOK
    q_all = nz * q_each

    def place(index):
        return lax.div(index, 2 * nx), lax.rem(lax.div(index, 2), nx), lax.rem(index, 2)

    def load(kind, c):
        src, dst = {
            "eo": lambda: (eig_out.at[pl.ds(c * out_step, out_step), :], v_eo.at[c]),
            "qg": lambda: (query_grads.at[:, pl.ds(c * out_step, out_step)], v_qg.at[c]),
            "g0": lambda: (grads.at[pl.ds(0, half), pl.ds(c * out_step, out_step)], v_g0.at[c]),
            "g1": lambda: (grads.at[pl.ds(half, half), pl.ds(c * out_step, out_step)], v_g1.at[c]),
            "ei": lambda: (eig_in.at[pl.ds(c * in_step, in_step), :], v_ei.at[c]),
            "qa": lambda: (query_acts.at[:, pl.ds(c * in_step, in_step)], v_qa.at[c]),
            "a": lambda: (acts.at[:, pl.ds(c * in_step, in_step)], v_a.at[c]),
        }[kind]()
        row = ("eo", "qg", "g0", "g1", "ei", "qa", "a").index(kind)
        return pltpu.make_async_copy(src, dst, load_sem.at[row, c])

    for c in range(n_in):
        load("ei", c).start()
        load("qa", c).start()
    for c in range(n_out):
        load("eo", c).start()
        load("qg", c).start()
    for c in range(n_in):
        load("a", c).start()
    for kind in ("g0", "g1"):
        for c in range(n_out):
            load(kind, c).start()
    own_level = pltpu.make_async_copy(
        eigenvalues.at[:, pl.ds(pl.multiple_of(x * wide, LANES), wide)], levels.at[x], load_sem.at[7, 0]
    )
    own_level.start()

    barrier = pltpu.get_barrier_semaphore()

    def greet(r, carry):
        oz, ox, os = place(lax.rem(me + r, n_all))
        pl.semaphore_signal(barrier, inc=1, device_id=(part, oz, ox, os), device_id_type=MESH)
        return carry

    lax.fori_loop(1, n_all, greet, 0)

    def along_x(kind, r, arriving=False):
        other = lax.rem(x + r, nx)
        back = lax.rem(x + nx - r, nx)
        src, dst = {
            "ev": lambda: (eigenvalues.at[:, pl.ds(pl.multiple_of(other * wide, LANES), wide)], levels),
            "qi": lambda: (send_qi.at[other], got_qi),
            "qo": lambda: (send_qo, got_qo),
            "ti": lambda: (send_ti.at[other], got_ti),
            "to0": lambda: (send_to0, got_to0),
            "to1": lambda: (send_to1, got_to1),
        }[kind]()
        row = ("ev", "qi", "qo", "ti", "to0", "to1").index(kind)

        def copy(slot):
            return pltpu.make_async_remote_copy(
                src_ref=src, dst_ref=dst.at[slot], send_sem=x_send.at[row, r], recv_sem=x_recv.at[row, r],
                device_id=(part, z, other, s), device_id_type=MESH,
            )

        return copy(back if arriving else x)

    def start_x(kind):
        for r in range(1, nx):
            along_x(kind, r).start()

    def wait_x(kind):
        for r in range(1, nx):
            along_x(kind, r, True).wait_recv()

    def summed(own, got):
        total = own
        for r in range(1, nx):
            total = total + got[lax.rem(x + nx - r, nx)].astype(f32)
        return total

    def rotate_out(kind, held, acc, first, last):
        def step(c, carry):
            if kind == "qg":
                load("eo", c).wait()
            load(kind, c).wait()
            acc[...] += dot(held[c], v_eo[c])
            return carry

        lax.fori_loop(first, last, step, 0)

    def rotate_in(kind, held, acc):
        acc[...] = jnp.zeros_like(acc)

        def step(c, carry):
            if kind == "qa":
                load("ei", c).wait()
            load(kind, c).wait()
            for j in range(nx):
                acc[j] += dot(held[c], v_ei[c, :, j * wide:(j + 1) * wide])
            return carry

        lax.fori_loop(0, n_in, step, 0)

    def along_z(kind, r, arriving=False):
        ref = que_out if kind == 0 else que_in
        other = lax.rem(z + r, nz)
        back = lax.rem(z + nz - r, nz)

        def copy(slot):
            return pltpu.make_async_remote_copy(
                src_ref=ref.at[slot], dst_ref=ref.at[slot], send_sem=z_send.at[kind, r], recv_sem=z_recv.at[kind, r],
                device_id=(part, other, x, s), device_id_type=MESH,
            )

        return copy(back if arriving else z)

    def start_z(kind):
        def one(r, carry):
            along_z(kind, r).start()
            return carry

        lax.fori_loop(1, nz, one, 0)

    acc_qo[...] = jnp.zeros_like(acc_qo)
    acc_to0[...] = jnp.zeros_like(acc_to0)
    acc_to1[...] = jnp.zeros_like(acc_to1)
    placed[...] = jnp.zeros_like(placed)
    rotate_in("qa", v_qa, acc_qi)
    send_qi[...] = acc_qi[...].astype(bf16)
    pl.semaphore_wait(barrier, n_all - 1)
    start_x("qi")
    rotate_out("qg", v_qg, acc_qo, 0, n_out // 2)
    wait_x("qi")
    que_in[z] = summed(acc_qi[x], got_qi).astype(bf16)
    start_z(1)
    rotate_out("qg", v_qg, acc_qo, n_out // 2, n_out)
    send_qo[...] = acc_qo[...].astype(bf16)
    start_x("qo")
    start_x("ev")

    rotate_in("a", v_a, acc_ti)
    send_ti[...] = acc_ti[...].astype(bf16)
    start_x("ti")
    rotate_out("g0", v_g0, acc_to0, 0, n_out // 2)
    wait_x("qo")
    que_out[z] = summed(acc_qo[...], got_qo).T.astype(bf16)
    start_z(0)
    rotate_out("g0", v_g0, acc_to0, n_out // 2, n_out)
    send_to0[...] = acc_to0[...].astype(bf16)
    start_x("to0")

    def to_core(kind, slot):
        ref = (tok_out0.at[slot], tok_out1.at[slot], tok_in.at[slot])[kind]
        return pltpu.make_async_remote_copy(
            src_ref=ref, dst_ref=ref, send_sem=core_send.at[kind], recv_sem=core_recv.at[kind],
            device_id=(part, z, x, 1 - s), device_id_type=MESH,
        )

    rotate_out("g1", v_g1, acc_to1, 0, n_out)
    send_to1[...] = acc_to1[...].astype(bf16)
    start_x("to1")
    wait_x("ti")
    tok_in[s] = summed(acc_ti[x], got_ti).astype(bf16)
    to_core(2, s).start()
    wait_x("to0")
    tok_out0[s] = summed(acc_to0[...], got_to0).T.astype(bf16)
    to_core(0, s).start()

    own_level.wait()
    wait_x("ev")
    levels[...] = 1.0 / (levels[...] + damping)
    q_batch = min(4, q_each)

    def damp(zb):
        lane = lax.broadcasted_iota(jnp.int32, (1, q_rows), 1)
        scale = levels[...].reshape(ks, wide)
        for k0 in range(0, q_each, q_batch):
            stack = []
            for k in range(k0, k0 + q_batch):
                keep = ((lane >= k * QTOK) & (lane < (k + 1) * QTOK)).astype(f32).astype(bf16)
                stack.append(que_out[zb] * keep)
            outer = dot(jnp.concatenate(stack, axis=0), que_in[zb])
            for i in range(q_batch):
                block = (outer[i * ks:(i + 1) * ks] * scale).astype(bf16)
                que_grad[:, zb * q_each + k0 + i] = block.reshape(ks // GROUP, GROUP, wide)

    damp(z)
    wait_x("to1")
    tok_out1[s] = summed(acc_to1[...], got_to1).T.astype(bf16)
    to_core(1, s).start()

    fold_row = lax.broadcasted_iota(jnp.int32, fold.shape, 0)
    fold_col = lax.broadcasted_iota(jnp.int32, fold.shape, 1)
    folding = jnp.zeros(fold.shape, f32)
    for d in range(doc_count):
        owner = own_ref[0, d]
        slot = jnp.int32(0)
        for e in range(d):
            slot = slot + jnp.where(own_ref[0, e] == owner, 1, 0)
        here = (fold_row == owner * PAD + slot) & (fold_col >= d * GROUP) & (fold_col < (d + 1) * GROUP)
        folding = jnp.where(here, 1.0, folding)
    fold[...] = folding

    for kind in range(3):
        to_core(kind, 1 - s).wait_recv()

    batch = min(4, doc_count)

    def documents(k, begin):
        ends = [begin]
        for i in range(batch):
            ends.append(ends[-1] + len_ref[0, k * batch + i])
        total = None
        for side in range(2):
            for h in range(2):
                at = lax.broadcasted_iota(jnp.int32, (1, half), 1) + (side * rows + h * half)
                stack = []
                for i in range(batch):
                    keep = ((at >= ends[i]) & (at < ends[i + 1])).astype(f32).astype(bf16)
                    stack.append(tok_out[h][side] * keep)
                term = dot(jnp.concatenate(stack, axis=0), tok_in[side, h * half:(h + 1) * half, :])
                total = term if total is None else total + term
        for i in range(batch):
            block = total[i * ks:(i + 1) * ks].astype(bf16)
            doc_grad[:, k * batch + i] = block.reshape(ks // GROUP, GROUP, wide)
        return ends[-1]

    lax.fori_loop(0, doc_count // batch, documents, jnp.int32(0))

    def damp_far(r, carry):
        along_z(0, r, True).wait_recv()
        along_z(1, r, True).wait_recv()
        damp(lax.rem(z + nz - r, nz))
        return carry

    lax.fori_loop(1, nz, damp_far, 0)

    pair[...] = jnp.zeros_like(pair)

    def pairs(g, carry):
        total = None
        for i in range(4):
            left = que_grad[g * 4 + i].reshape(q_all * GROUP, wide)
            right = doc_grad[g * 4 + i].reshape(doc_count * GROUP, wide)
            term = dot(left, right, ((1,), (1,)))
            total = term if total is None else total + term
        pair[...] += total
        return carry

    lax.fori_loop(0, ks // GROUP // 4, pairs, 0)
    row = lax.broadcasted_iota(jnp.int32, pair.shape, 0)
    col = lax.broadcasted_iota(jnp.int32, pair.shape, 1)
    same = jnp.where(lax.rem(row, GROUP) == lax.rem(col, GROUP), pair[...], 0.0)
    by_query = jnp.sum(same.reshape(q_all, GROUP, doc_count * GROUP), axis=1)
    highest = lax.Precision.HIGHEST
    placed[:, :, 0:q_all] = dot(fold[...], by_query, ((1,), (1,)), highest).reshape(nz, PAD, q_all)

    def to_owner(r):
        oz, ox, os = place(lax.rem(me + r, n_all))
        return pltpu.make_async_remote_copy(
            src_ref=placed.at[oz], dst_ref=table.at[x * 2 + s, z], send_sem=last_send.at[r], recv_sem=last_recv.at[r],
            device_id=(part, oz, ox, os), device_id_type=MESH,
        )

    def from_source(r):
        oz, ox, os = place(lax.rem(me + n_all - r, n_all))
        return pltpu.make_async_remote_copy(
            src_ref=placed.at[0], dst_ref=table.at[ox * 2 + os, oz], send_sem=last_send.at[r], recv_sem=last_recv.at[r],
            device_id=(part, oz, ox, os), device_id_type=MESH,
        )

    def start_last(r, carry):
        to_owner(r).start()
        return carry

    lax.fori_loop(1, n_all, start_last, 0)
    table[x * 2 + s, z] = placed[z]

    for kind in ("ev", "qi", "qo", "ti", "to0", "to1"):
        for r in range(1, nx):
            along_x(kind, r).wait_send()
    for kind in range(3):
        to_core(kind, s).wait_send()

    def sent_z(r, carry):
        along_z(0, r).wait_send()
        along_z(1, r).wait_send()
        return carry

    lax.fori_loop(1, nz, sent_z, 0)

    def finish_last(r, carry):
        from_source(r).wait_recv()
        to_owner(r).wait_send()
        return carry

    lax.fori_loop(1, n_all, finish_last, 0)

    width = out_ref.shape[1]
    block = x * 2 + s
    result = jnp.zeros((nz * PAD, width), f32)
    pick_row = lax.broadcasted_iota(jnp.int32, (LANES, width), 0)
    pick_col = lax.broadcasted_iota(jnp.int32, (LANES, width), 1)
    for side in range(2):
        total = table[side].reshape(nz * PAD, LANES)
        for ox in range(1, nx):
            total = total + table[ox * 2 + side].reshape(nz * PAD, LANES)
        query = lax.div(pick_row, q_each) * (2 * q_each) + side * q_each + lax.rem(pick_row, q_each)
        pick = ((query == block * width + pick_col) & (pick_row < q_all)).astype(f32)
        result = result + dot(total, pick, precision=highest)
    for zz in range(nz):
        out_ref[zz * capacity:(zz + 1) * capacity, :] = result[zz * PAD:zz * PAD + capacity, :]


def chunk(extent, most):
    return min(extent, most)


def per_device(acts, grads, eig_in, eig_out, query_acts, query_grads, eigenvalues, lengths, owner):
    nz, nx = lax.axis_size("dp"), lax.axis_size("tensor")
    rows, q_rows = acts.shape[0], query_acts.shape[0]
    ka, ks = eig_in.shape[1], eig_out.shape[1]
    wide = ka // nx
    in_step, out_step = chunk(acts.shape[1], 2048), chunk(grads.shape[1], 2048)
    n_in, n_out = acts.shape[1] // in_step, grads.shape[1] // out_step
    doc_count = lengths.shape[1]
    capacity = max(3, (doc_count + nz - 1) // nz)
    q_each = q_rows // QTOK
    q_all = nz * q_each
    n_all = nz * nx * 2
    width = q_all * 2 // (nx * 2)
    sizes = (nz, nx, n_in, n_out, in_step, out_step, doc_count, capacity)
    any_spec = pl.BlockSpec(memory_space=pl.ANY)
    smem = pl.BlockSpec(memory_space=pltpu.SMEM)
    dma = pltpu.SemaphoreType.DMA
    return pl.pallas_call(
        functools.partial(kernel, sizes),
        out_shape=jax.ShapeDtypeStruct((nz * capacity, width), f32),
        in_specs=[smem, smem] + [any_spec] * 7,
        out_specs=pl.BlockSpec(memory_space=pltpu.VMEM),
        scratch_shapes=[
            pltpu.VMEM((n_in, rows, in_step), bf16),
            pltpu.VMEM((n_out, rows // 2, out_step), bf16),
            pltpu.VMEM((n_out, rows // 2, out_step), bf16),
            pltpu.VMEM((n_in, in_step, ka), bf16),
            pltpu.VMEM((n_out, out_step, ks), bf16),
            pltpu.VMEM((n_in, q_rows, in_step), bf16),
            pltpu.VMEM((n_out, q_rows, out_step), bf16),
            pltpu.VMEM((nx, rows, wide), f32),
            pltpu.VMEM((rows // 2, ks), f32),
            pltpu.VMEM((rows // 2, ks), f32),
            pltpu.VMEM((nx, q_rows, wide), f32),
            pltpu.VMEM((q_rows, ks), f32),
            pltpu.VMEM((nx, rows, wide), bf16),
            pltpu.VMEM((rows // 2, ks), bf16),
            pltpu.VMEM((rows // 2, ks), bf16),
            pltpu.VMEM((nx, q_rows, wide), bf16),
            pltpu.VMEM((q_rows, ks), bf16),
            pltpu.VMEM((nx, rows, wide), bf16),
            pltpu.VMEM((nx, rows // 2, ks), bf16),
            pltpu.VMEM((nx, rows // 2, ks), bf16),
            pltpu.VMEM((nx, q_rows, wide), bf16),
            pltpu.VMEM((nx, q_rows, ks), bf16),
            pltpu.VMEM((2, rows, wide), bf16),
            pltpu.VMEM((2, ks, rows // 2), bf16),
            pltpu.VMEM((2, ks, rows // 2), bf16),
            pltpu.VMEM((nz, q_rows, wide), bf16),
            pltpu.VMEM((nz, ks, q_rows), bf16),
            pltpu.VMEM((nx, ks // nx, wide), f32),
            pltpu.VMEM((ks // GROUP, doc_count, GROUP, wide), bf16),
            pltpu.VMEM((ks // GROUP, q_all, GROUP, wide), bf16),
            pltpu.VMEM((q_all * GROUP, doc_count * GROUP), f32),
            pltpu.VMEM((nz * PAD, doc_count * GROUP), f32),
            pltpu.VMEM((nz, PAD, LANES), f32),
            pltpu.VMEM((nx * 2, nz, PAD, LANES), f32),
            dma((8, max(n_in, n_out))),
            dma((6, nx)),
            dma((6, nx)),
            dma((3,)),
            dma((3,)),
            dma((2, nz)),
            dma((2, nz)),
            dma((n_all,)),
            dma((n_all,)),
        ],
        compiler_params=pltpu.CompilerParams(
            collective_id=0, has_side_effects=True, vmem_limit_bytes=63 * 1024 * 1024
        ),
        cost_estimate=pl.CostEstimate(
            flops=2 * (rows + q_rows) * (acts.shape[1] * ka + grads.shape[1] * ks),
            bytes_accessed=2 * (rows + q_rows) * (acts.shape[1] + grads.shape[1]),
            transcendentals=0,
        ),
    )(
        lengths, owner.reshape(1, doc_count), acts, grads, eig_in, eig_out, query_acts, query_grads, eigenvalues
    )


def solution(mesh):
    return jax.shard_map(
        per_device,
        mesh=mesh,
        in_specs=(
            P(("parts", "dp", "seq"), "tensor"),
            P(("parts", "dp", "seq"), "tensor"),
            P("tensor", None),
            P("tensor", None),
            P(("parts", "dp", "seq"), "tensor"),
            P(("parts", "dp", "seq"), "tensor"),
            P("tensor", None),
            P(("parts", "dp"), None),
            P(("parts", "dp"), None, None),
        ),
        out_specs=P(("parts", "dp"), ("tensor", "seq")),
        check_vma=False,
    )
```

```python
import functools

import jax
import jax.numpy as jnp
from jax import lax
from jax.experimental import pallas as pl
from jax.experimental.pallas import tpu as pltpu
from jax.sharding import PartitionSpec as P

QTOK = 32
PAD = 8
LANES = 128
GROUP = 16


damping = 0.01
MESH = pl.DeviceIdType.MESH
f32, bf16 = jnp.float32, jnp.bfloat16


def dot(a, b, dims=((1,), (0,)), precision=None):
    return lax.dot_general(a, b, (dims, ((), ())), precision=precision, preferred_element_type=f32)


def kernel(
    sizes, len_ref, own_ref, acts, grads, eig_in, eig_out, query_acts, query_grads, eigenvalues, out_ref,
    v_a, v_g0, v_g1, v_ei, v_eo, v_qa, v_qg,
    acc_ti, acc_to0, acc_to1, acc_qi, acc_qo,
    send_ti, send_to0, send_to1, send_qi, send_qo,
    got_ti, got_to0, got_to1, got_qi, got_qo,
    tok_in, tok_out0, tok_out1, que_in, que_out,
    levels, doc_grad, que_grad, pair, fold, placed, table,
    load_sem, x_send, x_recv, core_send, core_recv, z_send, z_recv, last_send, last_recv,
):
    tok_out = (tok_out0, tok_out1)
    nz, nx, n_in, n_out, in_step, out_step, doc_count, capacity = sizes
    part, z, x, s = (lax.axis_index(name) for name in ("parts", "dp", "tensor", "seq"))
    n_all = nz * nx * 2
    me = (z * nx + x) * 2 + s
    rows, wide = acc_ti.shape[1:]
    ks = acc_to0.shape[1]
    half = rows // 2
    q_rows = acc_qo.shape[0]
    q_each = q_rows // QTOK
    q_all = nz * q_each

    def place(index):
        return lax.div(index, 2 * nx), lax.rem(lax.div(index, 2), nx), lax.rem(index, 2)

    def load(kind, c):
        src, dst = {
            "eo": lambda: (eig_out.at[pl.ds(c * out_step, out_step), :], v_eo.at[c]),
            "qg": lambda: (query_grads.at[:, pl.ds(c * out_step, out_step)], v_qg.at[c]),
            "g0": lambda: (grads.at[pl.ds(0, half), pl.ds(c * out_step, out_step)], v_g0.at[c]),
            "g1": lambda: (grads.at[pl.ds(half, half), pl.ds(c * out_step, out_step)], v_g1.at[c]),
            "ei": lambda: (eig_in.at[pl.ds(c * in_step, in_step), :], v_ei.at[c]),
            "qa": lambda: (query_acts.at[:, pl.ds(c * in_step, in_step)], v_qa.at[c]),
            "a": lambda: (acts.at[:, pl.ds(c * in_step, in_step)], v_a.at[c]),
        }[kind]()
        row = ("eo", "qg", "g0", "g1", "ei", "qa", "a").index(kind)
        return pltpu.make_async_copy(src, dst, load_sem.at[row, c])

    for c in range(n_in):
        load("ei", c).start()
        load("qa", c).start()
    for c in range(n_out):
        load("eo", c).start()
        load("qg", c).start()
    for c in range(n_in):
        load("a", c).start()
    for kind in ("g0", "g1"):
        for c in range(n_out):
            load(kind, c).start()
    own_level = pltpu.make_async_copy(
        eigenvalues.at[:, pl.ds(pl.multiple_of(x * wide, LANES), wide)], levels.at[x], load_sem.at[7, 0]
    )
    own_level.start()

    barrier = pltpu.get_barrier_semaphore()

    def greet(r, carry):
        oz, ox, os = place(lax.rem(me + r, n_all))
        pl.semaphore_signal(barrier, inc=1, device_id=(part, oz, ox, os), device_id_type=MESH)
        return carry

    lax.fori_loop(1, n_all, greet, 0)

    def along_x(kind, r, arriving=False):
        other = lax.rem(x + r, nx)
        back = lax.rem(x + nx - r, nx)
        src, dst = {
            "ev": lambda: (eigenvalues.at[:, pl.ds(pl.multiple_of(other * wide, LANES), wide)], levels),
            "qi": lambda: (send_qi.at[other], got_qi),
            "qo": lambda: (send_qo, got_qo),
            "ti": lambda: (send_ti.at[other], got_ti),
            "to0": lambda: (send_to0, got_to0),
            "to1": lambda: (send_to1, got_to1),
        }[kind]()
        row = ("ev", "qi", "qo", "ti", "to0", "to1").index(kind)

        def copy(slot):
            return pltpu.make_async_remote_copy(
                src_ref=src, dst_ref=dst.at[slot], send_sem=x_send.at[row, r], recv_sem=x_recv.at[row, r],
                device_id=(part, z, other, s), device_id_type=MESH,
            )

        return copy(back if arriving else x)

    def start_x(kind):
        for r in range(1, nx):
            along_x(kind, r).start()

    def wait_x(kind):
        for r in range(1, nx):
            along_x(kind, r, True).wait_recv()

    def summed(own, got):
        total = own
        for r in range(1, nx):
            total = total + got[lax.rem(x + nx - r, nx)].astype(f32)
        return total

    def rotate_out(kind, held, acc, first, last):
        def step(c, carry):
            if kind == "qg":
                load("eo", c).wait()
            load(kind, c).wait()
            acc[...] += dot(held[c], v_eo[c])
            return carry

        lax.fori_loop(first, last, step, 0)

    def rotate_in(kind, held, acc):
        acc[...] = jnp.zeros_like(acc)

        def step(c, carry):
            if kind == "qa":
                load("ei", c).wait()
            load(kind, c).wait()
            for j in range(nx):
                acc[j] += dot(held[c], v_ei[c, :, j * wide:(j + 1) * wide])
            return carry

        lax.fori_loop(0, n_in, step, 0)

    def along_z(kind, r, arriving=False):
        ref = que_out if kind == 0 else que_in
        other = lax.rem(z + r, nz)
        back = lax.rem(z + nz - r, nz)

        def copy(slot):
            return pltpu.make_async_remote_copy(
                src_ref=ref.at[slot], dst_ref=ref.at[slot], send_sem=z_send.at[kind, r], recv_sem=z_recv.at[kind, r],
                device_id=(part, other, x, s), device_id_type=MESH,
            )

        return copy(back if arriving else z)

    def start_z(kind):
        def one(r, carry):
            along_z(kind, r).start()
            return carry

        lax.fori_loop(1, nz, one, 0)

    acc_qo[...] = jnp.zeros_like(acc_qo)
    acc_to0[...] = jnp.zeros_like(acc_to0)
    acc_to1[...] = jnp.zeros_like(acc_to1)
    placed[...] = jnp.zeros_like(placed)
    pl.semaphore_wait(barrier, n_all - 1)
    start_x("ev")
    rotate_in("qa", v_qa, acc_qi)
    send_qi[...] = acc_qi[...].astype(bf16)
    start_x("qi")
    rotate_out("qg", v_qg, acc_qo, 0, n_out // 2)
    wait_x("qi")
    que_in[z] = summed(acc_qi[x], got_qi).astype(bf16)
    start_z(1)
    rotate_out("qg", v_qg, acc_qo, n_out // 2, n_out)
    send_qo[...] = acc_qo[...].astype(bf16)
    start_x("qo")

    rotate_in("a", v_a, acc_ti)
    send_ti[...] = acc_ti[...].astype(bf16)
    start_x("ti")
    rotate_out("g0", v_g0, acc_to0, 0, n_out // 2)
    wait_x("qo")
    que_out[z] = summed(acc_qo[...], got_qo).T.astype(bf16)
    start_z(0)
    rotate_out("g0", v_g0, acc_to0, n_out // 2, n_out)
    send_to0[...] = acc_to0[...].astype(bf16)
    start_x("to0")

    def to_core(kind, slot):
        ref = (tok_out0.at[slot], tok_out1.at[slot], tok_in.at[slot])[kind]
        return pltpu.make_async_remote_copy(
            src_ref=ref, dst_ref=ref, send_sem=core_send.at[kind], recv_sem=core_recv.at[kind],
            device_id=(part, z, x, 1 - s), device_id_type=MESH,
        )

    rotate_out("g1", v_g1, acc_to1, 0, n_out)
    send_to1[...] = acc_to1[...].astype(bf16)
    start_x("to1")
    wait_x("ti")
    tok_in[s] = summed(acc_ti[x], got_ti).astype(bf16)
    to_core(2, s).start()
    wait_x("to0")
    tok_out0[s] = summed(acc_to0[...], got_to0).T.astype(bf16)
    to_core(0, s).start()

    own_level.wait()
    wait_x("ev")
    levels[...] = 1.0 / (levels[...] + damping)
    q_batch = min(4, q_each)

    def damp(zb):
        lane = lax.broadcasted_iota(jnp.int32, (1, q_rows), 1)
        scale = levels[...].reshape(ks, wide)
        for k0 in range(0, q_each, q_batch):
            stack = []
            for k in range(k0, k0 + q_batch):
                keep = ((lane >= k * QTOK) & (lane < (k + 1) * QTOK)).astype(f32).astype(bf16)
                stack.append(que_out[zb] * keep)
            outer = dot(jnp.concatenate(stack, axis=0), que_in[zb])
            for i in range(q_batch):
                block = (outer[i * ks:(i + 1) * ks] * scale).astype(bf16)
                que_grad[:, zb * q_each + k0 + i] = block.reshape(ks // GROUP, GROUP, wide)

    damp(z)
    wait_x("to1")
    tok_out1[s] = summed(acc_to1[...], got_to1).T.astype(bf16)
    to_core(1, s).start()

    fold_row = lax.broadcasted_iota(jnp.int32, fold.shape, 0)
    fold_col = lax.broadcasted_iota(jnp.int32, fold.shape, 1)
    folding = jnp.zeros(fold.shape, f32)
    for d in range(doc_count):
        owner = own_ref[0, d]
        slot = jnp.int32(0)
        for e in range(d):
            slot = slot + jnp.where(own_ref[0, e] == owner, 1, 0)
        here = (fold_row == owner * PAD + slot) & (fold_col >= d * GROUP) & (fold_col < (d + 1) * GROUP)
        folding = jnp.where(here, 1.0, folding)
    fold[...] = folding

    def damp_far(r, carry):
        along_z(0, r, True).wait_recv()
        along_z(1, r, True).wait_recv()
        damp(lax.rem(z + nz - r, nz))
        return carry

    lax.fori_loop(1, nz, damp_far, 0)

    for kind in range(3):
        to_core(kind, 1 - s).wait_recv()

    batch = min(4, doc_count)

    def documents(k, begin):
        ends = [begin]
        for i in range(batch):
            ends.append(ends[-1] + len_ref[0, k * batch + i])
        total = None
        for side in range(2):
            for h in range(2):
                at = lax.broadcasted_iota(jnp.int32, (1, half), 1) + (side * rows + h * half)
                stack = []
                for i in range(batch):
                    keep = ((at >= ends[i]) & (at < ends[i + 1])).astype(f32).astype(bf16)
                    stack.append(tok_out[h][side] * keep)
                term = dot(jnp.concatenate(stack, axis=0), tok_in[side, h * half:(h + 1) * half, :])
                total = term if total is None else total + term
        for i in range(batch):
            block = total[i * ks:(i + 1) * ks].astype(bf16)
            doc_grad[:, k * batch + i] = block.reshape(ks // GROUP, GROUP, wide)
        return ends[-1]

    lax.fori_loop(0, doc_count // batch, documents, jnp.int32(0))

    pair[...] = jnp.zeros_like(pair)

    def pairs(g, carry):
        total = None
        for i in range(4):
            left = que_grad[g * 4 + i].reshape(q_all * GROUP, wide)
            right = doc_grad[g * 4 + i].reshape(doc_count * GROUP, wide)
            term = dot(left, right, ((1,), (1,)))
            total = term if total is None else total + term
        pair[...] += total
        return carry

    lax.fori_loop(0, ks // GROUP // 4, pairs, 0)
    row = lax.broadcasted_iota(jnp.int32, pair.shape, 0)
    col = lax.broadcasted_iota(jnp.int32, pair.shape, 1)
    same = jnp.where(lax.rem(row, GROUP) == lax.rem(col, GROUP), pair[...], 0.0)
    by_query = jnp.sum(same.reshape(q_all, GROUP, doc_count * GROUP), axis=1)
    highest = lax.Precision.HIGHEST
    placed[:, :, 0:q_all] = dot(fold[...], by_query, ((1,), (1,)), highest).reshape(nz, PAD, q_all)

    def to_owner(r):
        oz, ox, os = place(lax.rem(me + r, n_all))
        return pltpu.make_async_remote_copy(
            src_ref=placed.at[oz], dst_ref=table.at[x * 2 + s, z], send_sem=last_send.at[r], recv_sem=last_recv.at[r],
            device_id=(part, oz, ox, os), device_id_type=MESH,
        )

    def from_source(r):
        oz, ox, os = place(lax.rem(me + n_all - r, n_all))
        return pltpu.make_async_remote_copy(
            src_ref=placed.at[0], dst_ref=table.at[ox * 2 + os, oz], send_sem=last_send.at[r], recv_sem=last_recv.at[r],
            device_id=(part, oz, ox, os), device_id_type=MESH,
        )

    def start_last(r, carry):
        to_owner(r).start()
        return carry

    lax.fori_loop(1, n_all, start_last, 0)
    table[x * 2 + s, z] = placed[z]

    for kind in ("ev", "qi", "qo", "ti", "to0", "to1"):
        for r in range(1, nx):
            along_x(kind, r).wait_send()
    for kind in range(3):
        to_core(kind, s).wait_send()

    def sent_z(r, carry):
        along_z(0, r).wait_send()
        along_z(1, r).wait_send()
        return carry

    lax.fori_loop(1, nz, sent_z, 0)

    def finish_last(r, carry):
        from_source(r).wait_recv()
        to_owner(r).wait_send()
        return carry

    lax.fori_loop(1, n_all, finish_last, 0)

    width = out_ref.shape[1]
    block = x * 2 + s
    result = jnp.zeros((nz * PAD, width), f32)
    pick_row = lax.broadcasted_iota(jnp.int32, (LANES, width), 0)
    pick_col = lax.broadcasted_iota(jnp.int32, (LANES, width), 1)
    for side in range(2):
        total = table[side].reshape(nz * PAD, LANES)
        for ox in range(1, nx):
            total = total + table[ox * 2 + side].reshape(nz * PAD, LANES)
        query = lax.div(pick_row, q_each) * (2 * q_each) + side * q_each + lax.rem(pick_row, q_each)
        pick = ((query == block * width + pick_col) & (pick_row < q_all)).astype(f32)
        result = result + dot(total, pick, precision=highest)
    for zz in range(nz):
        out_ref[zz * capacity:(zz + 1) * capacity, :] = result[zz * PAD:zz * PAD + capacity, :]


def chunk(extent, most):
    return min(extent, most)


def per_device(acts, grads, eig_in, eig_out, query_acts, query_grads, eigenvalues, lengths, owner):
    nz, nx = lax.axis_size("dp"), lax.axis_size("tensor")
    rows, q_rows = acts.shape[0], query_acts.shape[0]
    ka, ks = eig_in.shape[1], eig_out.shape[1]
    wide = ka // nx
    in_step, out_step = chunk(acts.shape[1], 2048), chunk(grads.shape[1], 2048)
    n_in, n_out = acts.shape[1] // in_step, grads.shape[1] // out_step
    doc_count = lengths.shape[1]
    capacity = max(3, (doc_count + nz - 1) // nz)
    q_each = q_rows // QTOK
    q_all = nz * q_each
    n_all = nz * nx * 2
    width = q_all * 2 // (nx * 2)
    sizes = (nz, nx, n_in, n_out, in_step, out_step, doc_count, capacity)
    any_spec = pl.BlockSpec(memory_space=pl.ANY)
    smem = pl.BlockSpec(memory_space=pltpu.SMEM)
    dma = pltpu.SemaphoreType.DMA
    return pl.pallas_call(
        functools.partial(kernel, sizes),
        out_shape=jax.ShapeDtypeStruct((nz * capacity, width), f32),
        in_specs=[smem, smem] + [any_spec] * 7,
        out_specs=pl.BlockSpec(memory_space=pltpu.VMEM),
        scratch_shapes=[
            pltpu.VMEM((n_in, rows, in_step), bf16),
            pltpu.VMEM((n_out, rows // 2, out_step), bf16),
            pltpu.VMEM((n_out, rows // 2, out_step), bf16),
            pltpu.VMEM((n_in, in_step, ka), bf16),
            pltpu.VMEM((n_out, out_step, ks), bf16),
            pltpu.VMEM((n_in, q_rows, in_step), bf16),
            pltpu.VMEM((n_out, q_rows, out_step), bf16),
            pltpu.VMEM((nx, rows, wide), f32),
            pltpu.VMEM((rows // 2, ks), f32),
            pltpu.VMEM((rows // 2, ks), f32),
            pltpu.VMEM((nx, q_rows, wide), f32),
            pltpu.VMEM((q_rows, ks), f32),
            pltpu.VMEM((nx, rows, wide), bf16),
            pltpu.VMEM((rows // 2, ks), bf16),
            pltpu.VMEM((rows // 2, ks), bf16),
            pltpu.VMEM((nx, q_rows, wide), bf16),
            pltpu.VMEM((q_rows, ks), bf16),
            pltpu.VMEM((nx, rows, wide), bf16),
            pltpu.VMEM((nx, rows // 2, ks), bf16),
            pltpu.VMEM((nx, rows // 2, ks), bf16),
            pltpu.VMEM((nx, q_rows, wide), bf16),
            pltpu.VMEM((nx, q_rows, ks), bf16),
            pltpu.VMEM((2, rows, wide), bf16),
            pltpu.VMEM((2, ks, rows // 2), bf16),
            pltpu.VMEM((2, ks, rows // 2), bf16),
            pltpu.VMEM((nz, q_rows, wide), bf16),
            pltpu.VMEM((nz, ks, q_rows), bf16),
            pltpu.VMEM((nx, ks // nx, wide), f32),
            pltpu.VMEM((ks // GROUP, doc_count, GROUP, wide), bf16),
            pltpu.VMEM((ks // GROUP, q_all, GROUP, wide), bf16),
            pltpu.VMEM((q_all * GROUP, doc_count * GROUP), f32),
            pltpu.VMEM((nz * PAD, doc_count * GROUP), f32),
            pltpu.VMEM((nz, PAD, LANES), f32),
            pltpu.VMEM((nx * 2, nz, PAD, LANES), f32),
            dma((8, max(n_in, n_out))),
            dma((6, nx)),
            dma((6, nx)),
            dma((3,)),
            dma((3,)),
            dma((2, nz)),
            dma((2, nz)),
            dma((n_all,)),
            dma((n_all,)),
        ],
        compiler_params=pltpu.CompilerParams(
            collective_id=0, has_side_effects=True, vmem_limit_bytes=63 * 1024 * 1024
        ),
        cost_estimate=pl.CostEstimate(
            flops=2 * (rows + q_rows) * (acts.shape[1] * ka + grads.shape[1] * ks),
            bytes_accessed=2 * (rows + q_rows) * (acts.shape[1] + grads.shape[1]),
            transcendentals=0,
        ),
    )(
        lengths, owner.reshape(1, doc_count), acts, grads, eig_in, eig_out, query_acts, query_grads, eigenvalues
    )


def solution(mesh):
    return jax.shard_map(
        per_device,
        mesh=mesh,
        in_specs=(
            P(("parts", "dp", "seq"), "tensor"),
            P(("parts", "dp", "seq"), "tensor"),
            P("tensor", None),
            P("tensor", None),
            P(("parts", "dp", "seq"), "tensor"),
            P(("parts", "dp", "seq"), "tensor"),
            P("tensor", None),
            P(("parts", "dp"), None),
            P(("parts", "dp"), None, None),
        ),
        out_specs=P(("parts", "dp"), ("tensor", "seq")),
        check_vma=False,
    )
```
